32 devices in a mesh: groups: 2 (over y), slab: 4 (over z), coil: 2 (over x), pencil: 2 (over core).
Axes of the slice: x: 2, y: 2, z: 4, core: 2. Of those that a mesh axis runs over, the one named last changes fastest.
Arguments:
- estimate: float32 [2, 256, 128, 128], P(None, ('groups', 'slab', 'pencil'), 'coil'), parts along dimension 1, may hold values from -6 to 6
- coil_sens: bfloat16 [2, 8, 256, 128, 128], P(None, 'coil', ('groups', 'slab', 'pencil')), parts along dimension 2, may hold values from -3 to 3
- measured: bfloat16 [2, 8, 128, 256, 128], P(None, 'coil', None, ('groups', 'slab', 'pencil')), parts along dimension 3, may hold values from -4.1875 to 4.1875
- sampling: int32 [128, 256], P(None, ('groups', 'slab', 'pencil')), parts along dimension 1, may hold values 0 or 1
- step_size: float32 [1], replicated, may hold values from 0.2 to 2
- conv_in: bfloat16 [32, 2, 3, 3, 3], replicated, may hold values from -0.875 to 0.875
- bias_in: float32 [32], replicated, may hold values from -3 to 3
- conv_out: bfloat16 [2, 32, 3, 3, 3], replicated, may hold values from -0.21875 to 0.21875
Outputs:
- refined: float32 [2, 256, 128, 128], P(None, ('groups', 'slab', 'pencil'), 'coil'), parts along dimension 1
The draws below stay inside these ranges and needn't reach their ends.
There are 2 independent parts, one for each index of `groups`. The reference program is written for one: setup_inputs(seed, part) draws one part's arguments, and reference() takes and returns one part's arrays. A program takes and returns all parts, laid end to end along the dimension named above; an argument that names none is the same for every part. Nothing has to cross between parts.
All inputs are finite; a program needn't handle non-finite values. No bound on the sum of `sampling` on one device may be relied on, other than what follows from the above.
Results may differ from the reference program's by a relative error of at most 0.0014.
Values may be sent and summed in bfloat16 or wider, within the bound.
A program may use at most 192 MiB of HBM per device.

```python
import jax
import jax.numpy as jnp
from jax import lax

NX = 128
NY = 128
NZ = 128
NCOIL = 8
HID = 32


def set_ends(array, own_key, smallest, high):
    dims = array.shape
    spot = [jax.random.randint(jax.random.fold_in(own_key, axis), (), 0, dims[axis]) for axis in range(len(dims))]
    array = array.at[tuple(spot)].set(smallest)
    longest = dims.index(max(dims))
    spot[longest] = (spot[longest] + 1) % dims[longest]
    return array.at[tuple(spot)].set(high)


def block_scale(stream_key, shape, shards, smallest, high):
    def one(position, blocks):
        heights = jax.random.uniform(jax.random.fold_in(jax.random.fold_in(stream_key, 6), position), (blocks,), jnp.float32, smallest / len(shards), high / len(shards))
        return jnp.repeat(jnp.exp(heights), shape[position] // blocks).reshape((-1,) + (1,) * (len(shape) - position - 1))

    loudness = one(*shards[0])
    for cut in shards[1:]:
        loudness = loudness * one(*cut)
    return loudness


def normal_values(own_key, extent, width, bound, cuts=(), held_as=jnp.bfloat16):
    result = jax.random.normal(own_key, extent, jnp.float32) * width
    if len(cuts) > 0:
        result = block_scale(own_key, extent, cuts, -0.22, 0.18) * result
    return jnp.clip(result, min=-bound, max=bound).astype(held_as)


def setup_inputs(seed: int = 0, part: int = 0) -> dict:
    key_of = jax.random.split(jax.random.key(seed), 9)
    part_keys = jax.random.split(jax.random.fold_in(key_of[8], part), 9)
    estimate = normal_values(part_keys[0], (2, NZ, NY, NX), 1.0, 6.0, ((1, 8), (2, 2)), jnp.float32)
    coil_sens = normal_values(part_keys[1], (2, NCOIL, NZ, NY, NX), 0.5, 3.0, ((1, 2), (2, 8)))
    measured = normal_values(part_keys[2], (2, NCOIL, NZ, NY, NX), 0.7, 4.1875, ((1, 2), (3, 8)))
    sampling = set_ends((jax.random.randint(part_keys[3], (NZ, NY), 0, 3) < 1).astype(jnp.int32), jax.random.fold_in(part_keys[3], 1), 0, 1)
    step_size = jnp.clip(jax.random.uniform(key_of[4], (1,), jnp.float32, 0.2, 2.0), 0.2, 2.0)
    conv_in = normal_values(key_of[5], (HID, 2, 3, 3, 3), 54 ** -0.5, 0.875)
    bias_in = normal_values(key_of[6], (HID,), 0.5, 3.0, (), jnp.float32)
    conv_out = normal_values(key_of[7], (2, HID, 3, 3, 3), (HID * 27) ** -0.5, 0.21875)
    return {"estimate": estimate, "coil_sens": coil_sens, "measured": measured, "sampling": sampling, "step_size": step_size, "conv_in": conv_in, "bias_in": bias_in, "conv_out": conv_out}


PRECISE = lax.Precision.HIGHEST


def leaky_relu(values):
    return jnp.where(values > 0, values, 0.2 * values)


def convolve(volume, kernel):
    return lax.conv_general_dilated(volume[None], kernel, (1, 1, 1), "SAME", dimension_numbers=("NCDHW", "OIDHW", "NCDHW"), precision=PRECISE, preferred_element_type=volume.dtype)[0]


def reference(estimate, coil_sens, measured, sampling, step_size, conv_in, bias_in, conv_out):
    float_type = estimate.dtype
    current = estimate[0] + 1j * estimate[1]
    weights = sampling.astype(float_type)[:, :, None]

    def per_coil(running, pieces):
        coil_map, observed = pieces
        coil_map = coil_map.astype(float_type)
        observed = observed.astype(float_type)
        complex_map = coil_map[0] + 1j * coil_map[1]
        spectrum = jnp.fft.fftn(complex_map * current, norm="ortho")
        misfit = weights * (spectrum - (observed[0] + 1j * observed[1]))
        returned = jnp.fft.ifftn(misfit, norm="ortho")
        return running + jnp.conj(complex_map) * returned, None

    initial = jnp.zeros(current.shape, current.dtype)
    running, _ = lax.scan(per_coil, initial, (jnp.moveaxis(coil_sens, 1, 0), jnp.moveaxis(measured, 1, 0)))
    gradient = jnp.stack([jnp.real(running), jnp.imag(running)]).astype(float_type)
    rounded = lax.optimization_barrier(estimate.astype(jnp.bfloat16)).astype(float_type)
    hidden = leaky_relu(convolve(rounded, conv_in.astype(float_type)) + bias_in.astype(float_type)[:, None, None, None])
    hidden = lax.optimization_barrier(hidden.astype(jnp.bfloat16)).astype(float_type)
    regular = convolve(hidden, conv_out.astype(float_type))
    return estimate - step_size[0] * gradient - regular
```

```python
import jax
import jax.numpy as jnp
import numpy as np
from jax import lax
from jax.sharding import PartitionSpec as P

NY = 128
NZ = 128


PRECISE = lax.Precision.HIGH
LETTERS = "abcdefghij"
CHUNKS = 2


def extended(x, sides, width):
    for axis, dim in sides:
        size, length = (lax.axis_size(axis), x.shape[dim])
        up = [(i, (i + 1) % size) for i in range(size - 1)]
        down = [(j, i) for i, j in up]
        last = lax.slice_in_dim(x, length - width, length, axis=dim)
        initial = lax.slice_in_dim(x, 0, width, axis=dim)
        before = lax.ppermute(last, axis, up)
        after = lax.ppermute(initial, axis, down)
        x = jnp.concatenate([before, x, after], axis=dim)
    return x


def dft_block(length, inverse):
    indices = np.arange(length)
    angles = (indices[:, None] * indices[None, :] % length) * (2.0 * np.pi / length)
    cosine = np.cos(angles) / np.sqrt(length)
    sine = np.sin(angles) / np.sqrt(length)
    if inverse:
        sine = -sine
    block = np.stack([np.stack([cosine, sine], 1), np.stack([-sine, cosine], 1)])
    return jnp.asarray(block.astype(np.float32))


def transform(values, axis_pos, inverse):
    block = dft_block(values.shape[axis_pos], inverse)
    source = LETTERS[: values.ndim]
    target = "t" + source[1:axis_pos] + "z" + source[axis_pos + 1 :]
    return jnp.einsum(
        "tz" + source[0] + source[axis_pos] + "," + source + "->" + target, block, values, precision=PRECISE
    )


def pair_gather(x, axis, dim):
    if lax.axis_size(axis) != 2:
        return lax.all_gather(x, axis, axis=dim, tiled=True)
    other = lax.ppermute(x, axis, [(0, 1), (1, 0)])
    initial = lax.axis_index(axis) == 0
    return jnp.concatenate([jnp.where(initial, x, other), jnp.where(initial, other, x)], axis=dim)


def pair_scatter(x, axis, dim):
    if lax.axis_size(axis) != 2:
        return lax.psum_scatter(x, axis, scatter_dimension=dim, tiled=True)
    low, high = jnp.split(x, 2, axis=dim)
    initial = lax.axis_index(axis) == 0
    other = lax.ppermute(jnp.where(initial, high, low), axis, [(0, 1), (1, 0)])
    return jnp.where(initial, low, high) + other


def complex_product(operand, partner, conjugate):
    if conjugate:
        real_part = operand[0] * partner[0] + operand[1] * partner[1]
        imag_part = operand[0] * partner[1] - operand[1] * partner[0]
    else:
        real_part = operand[0] * partner[0] - operand[1] * partner[1]
        imag_part = operand[0] * partner[1] + operand[1] * partner[0]
    return jnp.stack([real_part, imag_part])


def banded(kernel, width):
    rows, ins, outs, _ = kernel.shape
    taps = jnp.repeat(kernel, width, axis=2)[:, :, None]
    x_in = lax.broadcasted_iota(jnp.int32, (width, outs * width), 0)
    x_out = lax.broadcasted_iota(jnp.int32, (width, outs * width), 1) % width
    offset = x_in - x_out + 1
    band = jnp.zeros((), kernel.dtype)
    for tap in range(3):
        band = jnp.where(offset == tap, taps[..., tap], band)
    return band.reshape(rows, ins * width, outs * width)


def row_conv(values, kernel):
    return lax.conv_general_dilated(
        values,
        kernel,
        (1,),
        "VALID",
        dimension_numbers=("NWC", "WIO", "NWC"),
        preferred_element_type=jnp.float32,
    )


def regularizer(estimate, conv_in, bias_in, conv_out):
    parts, z_local, y_local, x_count = estimate.shape
    plane_input = estimate.astype(jnp.bfloat16)
    rim_depth = 2
    framed = extended(plane_input, ((("slab", "pencil"), 1), ("coil", 2)), rim_depth)
    z_out = z_local + 2 * rim_depth - 2
    y_out = y_local + 2 * rim_depth - 2
    planes = jnp.transpose(framed, (1, 2, 0, 3)).reshape(z_out + 2, y_out + 2, parts * x_count)
    stacked = jnp.concatenate([planes[shift : shift + z_out] for shift in range(3)], axis=2)
    kernel_in = jnp.transpose(conv_in, (3, 2, 1, 0, 4)).reshape(3, 3 * parts, -1, 3)
    kernel_out = jnp.transpose(conv_out, (3, 1, 2, 0, 4)).reshape(3, -1, 3 * parts, 3)
    band_in = banded(kernel_in, x_count)
    band_out = banded(kernel_out, x_count)
    hidden = row_conv(stacked, band_in) + jnp.repeat(bias_in, x_count)
    hidden = jnp.where(hidden > 0, hidden, 0.2 * hidden)
    z_global = lax.axis_index(("slab", "pencil")) * z_local - 1 + lax.iota(jnp.int32, z_out)
    y_global = lax.axis_index("coil") * y_local - 1 + lax.iota(jnp.int32, y_out)
    inside = ((z_global >= 0) & (z_global < NZ))[:, None] & ((y_global >= 0) & (y_global < NY))[
        None, :
    ]
    framed_hidden = jnp.where(inside[:, :, None], hidden, 0.0).astype(jnp.bfloat16)
    products = row_conv(framed_hidden, band_out)
    result = sum(
        part[shift : shift + z_local] for shift, part in enumerate(jnp.split(products, 3, axis=2))
    )
    return jnp.transpose(result.reshape(z_local, y_local, parts, x_count), (2, 0, 1, 3))


def body(estimate, coil_sens, measured, sampling, step_size, conv_in, bias_in, conv_out):
    gathered = pair_gather(estimate, "coil", 2)
    weights = sampling.astype(jnp.float32)[None, None, :, :, None]
    lines = ("slab", "pencil")
    coils = coil_sens.shape[1]
    chunk = max(coils // CHUNKS, 1)
    partial_terms = jnp.zeros(gathered.shape, jnp.float32)
    for start in range(0, coils, chunk):
        coil_maps = coil_sens[:, start : start + chunk].astype(jnp.float32)
        observed = measured[:, start : start + chunk].astype(jnp.float32)
        coil_images = complex_product(coil_maps, gathered[:, None], False)
        spectra = transform(transform(coil_images, 4, False), 3, False)
        pencils = lax.all_to_all(
            spectra.astype(jnp.float16), lines, split_axis=3, concat_axis=2, tiled=True
        )
        spectra_full = transform(pencils.astype(jnp.float32), 2, False)
        misfit = weights * (spectra_full - observed)
        slab_view = lax.all_to_all(
            transform(misfit, 2, True).astype(jnp.float16), lines, split_axis=2, concat_axis=3, tiled=True
        )
        coil_back = transform(transform(slab_view.astype(jnp.float32), 3, True), 4, True)
        partial_terms = partial_terms + jnp.sum(complex_product(coil_maps, coil_back, True), axis=1)
    gradient = pair_scatter(partial_terms, "coil", 2)
    regular = regularizer(estimate, conv_in, bias_in, conv_out)
    return estimate - step_size[0] * gradient - regular


def solution(mesh):
    in_specs = (
        P(None, ("groups", "slab", "pencil"), "coil", None),
        P(None, "coil", ("groups", "slab", "pencil"), None, None),
        P(None, "coil", None, ("groups", "slab", "pencil"), None),
        P(None, ("groups", "slab", "pencil")),
        P(),
        P(),
        P(),
        P(),
    )
    out_specs = P(None, ("groups", "slab", "pencil"), "coil", None)
    return jax.shard_map(body, mesh=mesh, in_specs=in_specs, out_specs=out_specs, check_vma=False)
```

```python
import jax
import jax.numpy as jnp
import numpy as np
from jax import lax
from jax.sharding import PartitionSpec as P

NY = 128
NZ = 128


PRECISE = lax.Precision.HIGH
LETTERS = "abcdefghij"
CHUNKS = 2


def extended(x, sides, width):
    for axis, dim in sides:
        size, length = (lax.axis_size(axis), x.shape[dim])
        up = [(i, (i + 1) % size) for i in range(size - 1)]
        down = [(j, i) for i, j in up]
        last = lax.slice_in_dim(x, length - width, length, axis=dim)
        initial = lax.slice_in_dim(x, 0, width, axis=dim)
        before = lax.ppermute(last, axis, up)
        after = lax.ppermute(initial, axis, down)
        x = jnp.concatenate([before, x, after], axis=dim)
    return x


def dft_block(length, inverse):
    indices = np.arange(length)
    angles = (indices[:, None] * indices[None, :] % length) * (2.0 * np.pi / length)
    cosine = np.cos(angles) / np.sqrt(length)
    sine = np.sin(angles) / np.sqrt(length)
    if inverse:
        sine = -sine
    block = np.stack([np.stack([cosine, sine], 1), np.stack([-sine, cosine], 1)])
    return jnp.asarray(block.astype(np.float32))


def transform(values, axis_pos, inverse):
    block = dft_block(values.shape[axis_pos], inverse)
    source = LETTERS[: values.ndim]
    target = "t" + source[1:axis_pos] + "z" + source[axis_pos + 1 :]
    return jnp.einsum(
        "tz" + source[0] + source[axis_pos] + "," + source + "->" + target, block, values, precision=PRECISE
    )


def pair_gather(x, axis, dim, beside):
    if lax.axis_size(axis) != 2:
        return lax.all_gather(x, axis, axis=dim, tiled=True), beside
    other, beside = lax.optimization_barrier((lax.ppermute(x, axis, [(0, 1), (1, 0)]), beside))
    initial = lax.axis_index(axis) == 0
    return jnp.concatenate([jnp.where(initial, x, other), jnp.where(initial, other, x)], axis=dim), beside


def pair_scatter(x, axis, dim):
    if lax.axis_size(axis) != 2:
        return lax.psum_scatter(x, axis, scatter_dimension=dim, tiled=True)
    low, high = jnp.split(x, 2, axis=dim)
    initial = lax.axis_index(axis) == 0
    sent = (jnp.where(initial, high, low) * (1 / 64)).astype(jnp.float16)
    other = lax.ppermute(sent, axis, [(0, 1), (1, 0)])
    return jnp.where(initial, low, high) + other.astype(jnp.float32) * 64.0


def complex_product(operand, partner, conjugate):
    if conjugate:
        real_part = operand[0] * partner[0] + operand[1] * partner[1]
        imag_part = operand[0] * partner[1] - operand[1] * partner[0]
    else:
        real_part = operand[0] * partner[0] - operand[1] * partner[1]
        imag_part = operand[0] * partner[1] + operand[1] * partner[0]
    return jnp.stack([real_part, imag_part])


def banded(kernel, width):
    rows, ins, outs, _ = kernel.shape
    taps = jnp.repeat(kernel, width, axis=2)[:, :, None]
    x_in = lax.broadcasted_iota(jnp.int32, (width, outs * width), 0)
    x_out = lax.broadcasted_iota(jnp.int32, (width, outs * width), 1) % width
    offset = x_in - x_out + 1
    band = jnp.zeros((), kernel.dtype)
    for tap in range(3):
        band = jnp.where(offset == tap, taps[..., tap], band)
    return band.reshape(rows, ins * width, outs * width)


def row_conv(values, kernel):
    return lax.conv_general_dilated(
        values,
        kernel,
        (1,),
        "VALID",
        dimension_numbers=("NWC", "WIO", "NWC"),
        preferred_element_type=jnp.float32,
    )


def band_first(conv_in, x_count):
    hidden_count, parts = conv_in.shape[:2]
    kernel = jnp.transpose(conv_in, (3, 2, 1, 0, 4)).reshape(3, 3 * parts, hidden_count, 3)
    return banded(kernel, x_count)


def band_second(conv_out, x_count):
    parts, hidden_count = conv_out.shape[:2]
    kernel = jnp.transpose(conv_out, (3, 1, 2, 0, 4)).reshape(3, hidden_count, 3 * parts, 3)
    return banded(kernel, x_count)


def framed_volume(estimate):
    return extended(estimate.astype(jnp.bfloat16), ((("slab", "pencil"), 1), ("coil", 2)), 2)


def stacked_planes(framed):
    parts, z_framed, y_framed, x_count = framed.shape
    planes = jnp.transpose(framed, (1, 2, 0, 3)).reshape(z_framed, y_framed, parts * x_count)
    return jnp.concatenate([planes[shift : shift + z_framed - 2] for shift in range(3)], axis=2)


def first_layer(stacked, band_in, bias_in, x_count):
    z_out, y_out = stacked.shape[0], stacked.shape[1] - 2
    hidden = row_conv(stacked, band_in) + jnp.repeat(bias_in, x_count)
    hidden = jnp.where(hidden > 0, hidden, 0.2 * hidden)
    z_global = lax.axis_index(("slab", "pencil")) * (z_out - 2) - 1 + lax.iota(jnp.int32, z_out)
    y_global = lax.axis_index("coil") * (y_out - 2) - 1 + lax.iota(jnp.int32, y_out)
    inside = ((z_global >= 0) & (z_global < NZ))[:, None] & ((y_global >= 0) & (y_global < NY))[
        None, :
    ]
    return jnp.where(inside[:, :, None], hidden, 0.0).astype(jnp.bfloat16)


def second_layer(hidden, band_out, shape):
    parts, z_local, y_local, x_count = shape
    products = row_conv(hidden, band_out)
    result = sum(
        part[shift : shift + z_local] for shift, part in enumerate(jnp.split(products, 3, axis=2))
    )
    return jnp.transpose(result.reshape(z_local, y_local, parts, x_count), (2, 0, 1, 3))


def body(estimate, coil_sens, measured, sampling, step_size, conv_in, bias_in, conv_out):
    together = lax.optimization_barrier
    x_count = estimate.shape[3]
    band_in = band_first(conv_in, x_count)
    framed = framed_volume(estimate)
    gathered, band_in = pair_gather(estimate, "coil", 2, band_in)
    gathered, framed, conv_out = together((gathered, framed, conv_out))
    band_out = band_second(conv_out, x_count)
    stacked = stacked_planes(framed)
    weights = sampling.astype(jnp.float32)[None, None, :, :, None]
    lines = ("slab", "pencil")
    chunk = max(coil_sens.shape[1] // CHUNKS, 1)
    starts = range(0, coil_sens.shape[1], chunk)
    maps = [coil_sens[:, start : start + chunk] for start in starts]
    pencils = []
    for coil_maps in maps:
        coil_images = complex_product(coil_maps.astype(jnp.float32), gathered[:, None], False)
        spectra = transform(transform(coil_images, 4, False), 3, False)
        pencils.append(
            lax.all_to_all(spectra.astype(jnp.float16), lines, split_axis=3, concat_axis=2, tiled=True)
        )
    pencils[0], band_out, stacked = together((pencils[0], band_out, stacked))
    returned = []
    for start, lines_full in zip(starts, pencils):
        observed = measured[:, start : start + chunk].astype(jnp.float32)
        misfit = weights * (transform(lines_full.astype(jnp.float32), 2, False) - observed)
        returned.append(transform(misfit, 2, True).astype(jnp.float16))
    returned[-1], stacked = together((returned[-1], stacked))
    hidden = first_layer(stacked, band_in, bias_in, x_count)
    views = [lax.all_to_all(r, lines, split_axis=2, concat_axis=3, tiled=True) for r in returned]
    views[0], hidden = together((views[0], hidden))
    regular = second_layer(hidden, band_out, estimate.shape)
    views[-1], regular = together((views[-1], regular))
    partial_terms = jnp.zeros(gathered.shape, jnp.float32)
    for coil_maps, view in zip(maps, views):
        coil_back = transform(transform(view.astype(jnp.float32), 3, True), 4, True)
        terms = complex_product(coil_maps.astype(jnp.float32), coil_back, True)
        partial_terms = partial_terms + jnp.sum(terms, axis=1)
    gradient = pair_scatter(partial_terms, "coil", 2)
    return estimate - step_size[0] * gradient - regular


def solution(mesh):
    in_specs = (
        P(None, ("groups", "slab", "pencil"), "coil", None),
        P(None, "coil", ("groups", "slab", "pencil"), None, None),
        P(None, "coil", None, ("groups", "slab", "pencil"), None),
        P(None, ("groups", "slab", "pencil")),
        P(),
        P(),
        P(),
        P(),
    )
    out_specs = P(None, ("groups", "slab", "pencil"), "coil", None)
    return jax.shard_map(body, mesh=mesh, in_specs=in_specs, out_specs=out_specs, check_vma=False)
```
